128 devices in a mesh: row: 16 (over x, z_lo, core), col: 8 (over z_hi, y).
Axes of the slice: x: 4, y: 4, z: 4 (z_hi: 2, z_lo: 2; z = z_hi * 2 + z_lo), core: 2. Of those that a mesh axis runs over, the one named last changes fastest.
Arguments:
- pair: bfloat16 [1024, 1024, 128], P('row', 'col'), may hold values from -6 to 6
- chain_index: int32 [1024], replicated, may hold values from 0 to 3, never falling along the last dimension, each value on 1 to 512 neighbouring positions
- norm_gain: float32 [2, 2, 128], replicated, may hold values from 0.1 to 1.9
- norm_shift: float32 [2, 2, 128], replicated, may hold values from -1.5 to 1.5
- w_in: bfloat16 [2, 128, 5, 128], replicated, may hold values from -0.5 to 0.5
- b_in: float32 [2, 5, 128], replicated, may hold values from -1.5 to 1.5
- w_out: bfloat16 [2, 128, 128], replicated, may hold values from -0.5 to 0.5
- b_out: float32 [2, 128], replicated, may hold values from -3 to 3
Outputs:
- updated: bfloat16 [1024, 1024, 128], P('row', 'col')
The draws below stay inside these ranges and needn't reach their ends.
Inputs may be any that keep to these rules, and one draw needn't show every extreme that they name: `chain_index`: chain numbers never fall along the residues; each chain holds 1 to 512 residues, and one holds exactly 512.
All inputs are finite; a program needn't handle non-finite values.
Results may differ from the reference program's by a relative error of at most 0.007.
Values may be sent and summed in bfloat16 or wider, within the bound.
A program may use at most 64 MiB of HBM per device.

```python
import math
import jax
import jax.numpy as jnp
import numpy as np
from jax import lax

CH = 128
NCHAIN = 4
N = 1024
N_ROW = 16


def draw_pair(key, part):
    key = jax.random.fold_in(key, 11)
    values = jnp.clip(jax.random.normal(key, (N, N, CH), jnp.float32), -6.0, 6.0)
    return values.astype(jnp.bfloat16)


def draw_norm_shift(key, part):
    key = jax.random.fold_in(key, 23)
    scales = jnp.array([0.04, 0.5], jnp.float32)[None, :, None]
    values = jnp.clip(jax.random.normal(key, (2, 2, CH), jnp.float32), -3.0, 3.0)
    return values * scales


def draw_b_in(key, part):
    key = jax.random.fold_in(key, 37)
    scales = jnp.array([0.5, 0.04, 0.5, 0.04, 0.5], jnp.float32)[None, :, None]
    values = jnp.clip(jax.random.normal(key, (2, 5, CH), jnp.float32), -3.0, 3.0)
    return values * scales


def split_up(number_of, total, bound, skew):
    loads = [(1 << 20) // math.isqrt(grade ** skew) + 1 for grade in range(2, number_of + 1)]
    surplus, holding = total - bound - (number_of - 1), [1] * (number_of - 1)
    while surplus > 0:
        free = [i for i in range(number_of - 1) if holding[i] < bound]
        pool, left = sum([loads[i] for i in free]), surplus
        for i in free:
            extra = min(bound - holding[i], max(1, left * loads[i] // pool), surplus)
            holding[i] = holding[i] + extra
            surplus = surplus - extra
    return np.array([bound] + holding)


def ragged(stream_key, number_of, total, bound, slope):
    if number_of == 2:
        one = jax.random.randint(stream_key, (), max(1, total - bound), min(bound, total - 1) + 1)
        return jnp.stack([one, total - one])
    tallies = jnp.asarray(split_up(number_of, total, bound, slope), jnp.int32)
    couples = (number_of - 1) // 2
    source_of, receiver = tallies[1:1 + 2 * couples:2], tallies[2:2 + 2 * couples:2]
    room = jnp.minimum(source_of - 1, bound - receiver)
    moved = jax.random.randint(jax.random.fold_in(stream_key, 1), (couples,), 0, 1 << 20) % (room + 1)
    tallies = tallies.at[1:1 + 2 * couples:2].set(source_of - moved).at[2:2 + 2 * couples:2].set(receiver + moved)
    return tallies[jax.random.permutation(jax.random.fold_in(stream_key, 2), number_of)]


def noise(rng, shape, width, bound, kind=jnp.bfloat16):
    return jnp.clip(width * jax.random.normal(rng, shape, jnp.float32), -bound, bound).astype(kind)


def setup_inputs(seed: int = 0) -> dict:
    arg_keys = jax.random.split(jax.random.key(seed), 9)
    return {
        "pair": draw_pair(jax.random.fold_in(arg_keys[8], 71), 0),
        "chain_index": jnp.searchsorted(jnp.cumsum(ragged(arg_keys[1], NCHAIN, N, N // 2, 2)), jnp.arange(N), side="right").astype(jnp.int32),
        "norm_gain": jnp.clip(1.0 + 0.18 * jax.random.normal(arg_keys[2], (2, 2, CH), jnp.float32), 0.1, 1.9),
        "norm_shift": draw_norm_shift(jax.random.fold_in(arg_keys[8], 71), 0),
        "w_in": noise(arg_keys[4], (2, CH, 5, CH), CH ** -0.5, 0.5),
        "b_in": draw_b_in(jax.random.fold_in(arg_keys[8], 71), 0),
        "w_out": noise(arg_keys[6], (2, CH, CH), CH ** -0.5, 0.5),
        "b_out": noise(arg_keys[7], (2, CH), 0.5, 3.0, jnp.float32),
    }


EPS = 1e-05

def normalize(values, gain, shift, axis):
    mean = lax.optimization_barrier(jnp.mean(values, axis=axis, keepdims=True))
    spread = lax.optimization_barrier(jnp.mean(jnp.square(values - mean), axis=axis, keepdims=True))
    return (values - mean) * lax.rsqrt(spread + EPS) * gain + shift

def project_rows(rows, valid_rows, valid, gain, shift, weights, biases):
    normed = normalize(rows.astype(jnp.float32), gain, shift, -1).astype(jnp.bfloat16)
    count = rows.shape[0]
    proj = jnp.dot(normed.reshape(-1, CH), weights[:, :4].reshape(CH, 4 * CH), preferred_element_type=jnp.float32)
    proj = proj.reshape(count, N, 4, CH) + biases[:4]
    mask = valid_rows[:, None] * valid[None, :]
    gated = jax.nn.sigmoid(proj[:, :, 0::2]) * proj[:, :, 1::2] * mask[:, :, None, None]
    return gated.astype(jnp.bfloat16)

def update(pair, valid, gain, shift, weights, biases, w_last, b_last, incoming):
    blocks = pair.reshape(N_ROW, N // N_ROW, N, CH)
    valid_blocks = valid.reshape(N_ROW, N // N_ROW)
    gated = lax.map(lambda item: project_rows(item[0], item[1], valid, gain[0], shift[0], weights, biases), (blocks, valid_blocks))
    gated = gated.reshape(N, N, 2, CH)
    lefts = jnp.transpose(gated[:, :, 0], (2, 0, 1))
    rights = jnp.transpose(gated[:, :, 1], (2, 0, 1))

    def contract(item):
        left, right = item
        if incoming:
            return jnp.dot(left.T, right, preferred_element_type=jnp.float32).astype(jnp.bfloat16)
        return jnp.dot(left, right.T, preferred_element_type=jnp.float32).astype(jnp.bfloat16)
    mixed = lax.map(contract, (lefts, rights))
    mixed_blocks = jnp.transpose(mixed.reshape(CH, N_ROW, N // N_ROW, N), (1, 0, 2, 3))

    def finish(item):
        block, mixed_block = item
        count = block.shape[0]
        normed = normalize(block.astype(jnp.float32), gain[0], shift[0], -1).astype(jnp.bfloat16)
        gate = jax.nn.sigmoid(jnp.dot(normed.reshape(-1, CH), weights[:, 4], preferred_element_type=jnp.float32).reshape(count, N, CH) + biases[4])
        hidden = normalize(mixed_block.astype(jnp.float32), gain[1][:, None, None], shift[1][:, None, None], 0).astype(jnp.bfloat16)
        out = jnp.dot(hidden.reshape(CH, -1).T, w_last, preferred_element_type=jnp.float32).reshape(count, N, CH) + b_last
        return (block.astype(jnp.float32) + gate * out).astype(jnp.bfloat16)
    return lax.map(finish, (blocks, mixed_blocks)).reshape(N, N, CH)

def reference(pair, chain_index, norm_gain, norm_shift, w_in, b_in, w_out, b_out):
    valid = (chain_index < NCHAIN - 1).astype(jnp.float32)
    current = pair
    for layer in range(2):
        current = update(current, valid, norm_gain[layer], norm_shift[layer], w_in[layer], b_in[layer], w_out[layer], b_out[layer], layer == 1)
    return current
```

```python
import jax
import jax.numpy as jnp
from jax import lax
from jax.experimental import pallas as pl
from jax.experimental.pallas import tpu as pltpu
from jax.sharding import PartitionSpec as P

NCHAIN = 4
N = 1024
ROWS = 16
COLS = 8
DEVICES = ROWS * COLS
STRIDE = 31
MESH = pl.DeviceIdType.MESH


EPS = 1e-05


def normalize(values, gain, shift, axis):
    mean = jnp.mean(values, axis=axis, keepdims=True)
    spread = jnp.mean(jnp.square(values - mean), axis=axis, keepdims=True)
    return (values - mean) * lax.rsqrt(spread + EPS) * gain + shift


def partner(step):
    code = (STRIDE * step) % DEVICES
    dx, dcore = code % 4, code // 64
    dy = (code // 4 + 2 * dx) % 4
    dz = (code // 16 + 2 * (code // 4)) % 4
    row, col = lax.axis_index("row"), lax.axis_index("col")
    x = (row // 4 + dx) % 4
    y = (col % 4 + dy) % 4
    z = (col // 4 * 2 + row // 2 % 2 + dz) % 4
    core = (row % 2 + dcore) % 2
    return x * 4 + z % 2 * 2 + core, z // 2 * 4 + y


def exchange_kernel(src_ref, dst_ref, send_sem, recv_sem):
    me = lax.axis_index("row") * COLS + lax.axis_index("col")
    barrier = pltpu.get_barrier_semaphore()

    @pl.loop(1, DEVICES)
    def _(step):
        pl.semaphore_signal(barrier, inc=1, device_id=partner(step), device_id_type=MESH)

    pl.semaphore_wait(barrier, DEVICES - 1)

    @pl.loop(1, DEVICES)
    def _(step):
        row, col = partner(step)
        pltpu.make_async_remote_copy(
            src_ref=src_ref.at[row * COLS + col],
            dst_ref=dst_ref.at[me],
            send_sem=send_sem,
            recv_sem=recv_sem,
            device_id=(row, col),
            device_id_type=MESH,
        ).start()

    pltpu.make_async_copy(src_ref.at[me], dst_ref.at[me], recv_sem).start()
    pltpu.make_async_copy(src_ref, dst_ref, recv_sem).wait()
    others = pl.ds(0, DEVICES - 1)
    pltpu.make_async_copy(src_ref.at[others], dst_ref.at[others], send_sem).wait()


def exchange(blocks, collective_id):
    return pl.pallas_call(
        exchange_kernel,
        out_shape=jax.ShapeDtypeStruct(blocks.shape, blocks.dtype),
        in_specs=[pl.BlockSpec(memory_space=pltpu.VMEM)],
        out_specs=pl.BlockSpec(memory_space=pltpu.VMEM),
        scratch_shapes=[pltpu.SemaphoreType.DMA, pltpu.SemaphoreType.DMA],
        compiler_params=pltpu.CompilerParams(
            collective_id=collective_id, has_side_effects=True, vmem_limit_bytes=32 << 20
        ),
    )(blocks)


def spread_out(gated):
    blocks = exchange(jnp.transpose(gated, (1, 0, 2, 3)), 1)
    blocks = blocks.reshape(ROWS, COLS, 2, blocks.shape[2], blocks.shape[3])
    whole = jnp.transpose(blocks, (2, 0, 3, 1, 4))
    return whole.reshape(2, 1, N, N)


def bring_back(mixed):
    blocks = mixed.reshape(ROWS, N // ROWS, COLS, N // COLS)
    blocks = jnp.transpose(blocks, (0, 2, 1, 3)).reshape(DEVICES, N // ROWS, N // COLS)
    return exchange(blocks, 2)


def local(pair, chain_index, norm_gain, norm_shift, w_in, b_in, w_out, b_out):
    rows = pair.shape[0]
    cols = pair.shape[1]
    valid = (chain_index < NCHAIN - 1).astype(jnp.float32)
    row_valid = lax.dynamic_slice_in_dim(valid, lax.axis_index("row") * rows, rows)
    col_valid = lax.dynamic_slice_in_dim(valid, lax.axis_index("col") * cols, cols)
    mask = row_valid[:, None] * col_valid[None, :]
    current = pair
    for layer in range(2):
        normed = normalize(
            current.astype(jnp.float32), norm_gain[layer, 0], norm_shift[layer, 0], -1
        ).astype(jnp.bfloat16)
        halves = []
        for half in range(2):
            gate_part = jnp.einsum(
                "ijd,dc->cij", normed, w_in[layer, :, 2 * half], preferred_element_type=jnp.float32
            )
            gate_part = gate_part + b_in[layer, 2 * half][:, None, None]
            value_part = jnp.einsum(
                "ijd,dc->cij",
                normed,
                w_in[layer, :, 2 * half + 1],
                preferred_element_type=jnp.float32,
            )
            value_part = value_part + b_in[layer, 2 * half + 1][:, None, None]
            halves.append((jax.nn.sigmoid(gate_part) * value_part * mask).astype(jnp.bfloat16))
        gated = jnp.stack(halves)
        gate = jax.nn.sigmoid(
            jnp.einsum("ijd,dc->ijc", normed, w_in[layer, :, 4], preferred_element_type=jnp.float32)
            + b_in[layer, 4]
        )
        whole = spread_out(gated)
        if layer == 0:
            mixed = jnp.einsum(
                "cik,cjk->cij", whole[0], whole[1], preferred_element_type=jnp.float32
            )
        else:
            mixed = jnp.einsum(
                "cki,ckj->cij", whole[0], whole[1], preferred_element_type=jnp.float32
            )
        mixed = mixed.astype(jnp.bfloat16)
        tile_mixed = bring_back(mixed)
        hidden = normalize(
            tile_mixed.astype(jnp.float32),
            norm_gain[layer, 1][:, None, None],
            norm_shift[layer, 1][:, None, None],
            0,
        ).astype(jnp.bfloat16)
        out = (
            jnp.einsum("cij,cd->ijd", hidden, w_out[layer], preferred_element_type=jnp.float32)
            + b_out[layer]
        )
        current = (current.astype(jnp.float32) + gate * out).astype(jnp.bfloat16)
    return current


def solution(mesh):
    in_specs = (P("row", "col", None), P(), P(), P(), P(), P(), P(), P())
    out_specs = P("row", "col", None)
    return jax.shard_map(local, mesh=mesh, in_specs=in_specs, out_specs=out_specs, check_vma=False)
```

```python
import jax
import jax.numpy as jnp
from jax import lax
from jax.experimental import pallas as pl
from jax.experimental.pallas import tpu as pltpu
from jax.sharding import PartitionSpec as P

NCHAIN = 4
N = 1024
CH = 128
ROWS = 16
COLS = 8
DEVICES = ROWS * COLS
TILE_I = N // ROWS
TILE_J = N // COLS
PHASES = 4
BAND = TILE_I // PHASES
STRIDE = 31
MESH = pl.DeviceIdType.MESH
EPS = 1e-05


def partner(step, row, col):
    code = (STRIDE * step) & (DEVICES - 1)
    low, mid = code, code >> 2
    x = ((row >> 2) + low) & 3
    y = (col + mid + 2 * low) & 3
    z = (2 * (col >> 2) + ((row >> 1) & 1) + (code >> 4) + 2 * mid) & 3
    core = (row + (code >> 6)) & 1
    return 4 * x + 2 * (z & 1) + core, 4 * (z >> 1) + y


def dot(left, right, left_dim, right_dim):
    return lax.dot_general(
        left, right, (((left_dim,), (right_dim,)), ((), ())), preferred_element_type=jnp.float32
    )


def normalize(values, gain, shift, axis):
    mean = jnp.mean(values, axis=axis, keepdims=True)
    centred = values - mean
    spread = jnp.mean(jnp.square(centred), axis=axis, keepdims=True)
    return centred * lax.rsqrt(spread + EPS) * gain + shift


def kernel(
    pair_ref,
    mask_ref,
    w_in_ref,
    b_in_ref,
    w_gate_ref,
    b_gate_ref,
    gain_ref,
    shift_ref,
    hidden_gain_ref,
    hidden_shift_ref,
    w_out_ref,
    b_out_ref,
    out_ref,
    current,
    normed,
    gate,
    wide,
    edges_out,
    edges_in,
    mixed_out,
    mixed_in,
    load_sem,
    edge_send,
    edge_recv,
    mixed_send,
    mixed_recv,
    store_sem,
):
    row, col = lax.axis_index("row"), lax.axis_index("col")
    me = row * COLS + col
    barrier = pltpu.get_barrier_semaphore()

    def band_pairs(band):
        return pl.ds(pl.multiple_of(band * (BAND * TILE_J), BAND * TILE_J), BAND * TILE_J)

    def band_rows(band):
        return pl.ds(pl.multiple_of(band * BAND, BAND), BAND)

    def load(band):
        pairs = band_pairs(band)
        return pltpu.make_async_copy(pair_ref.at[pairs], current.at[pairs], load_sem.at[band])

    def store(band):
        pairs = band_pairs(band)
        return pltpu.make_async_copy(current.at[pairs], out_ref.at[pairs], store_sem.at[band])

    for band in range(PHASES):
        load(band).start()

    @pl.loop(1, DEVICES)
    def _(step):
        pl.semaphore_signal(barrier, inc=1, device_id=partner(step, row, col), device_id_type=MESH)

    def project(layer, band):
        @pl.loop(0, BAND)
        def _(i):
            line = band * BAND + i
            pairs = pl.ds(pl.multiple_of(line * TILE_J, TILE_J), TILE_J)
            values = normalize(
                current[pairs, :].astype(jnp.float32), gain_ref[layer], shift_ref[layer], -1
            ).astype(jnp.bfloat16)
            normed[pairs, :] = values
            mask = mask_ref[pl.ds(line, 1), :]
            for half in range(2):
                first, second = pl.ds(2 * half * CH, CH), pl.ds((2 * half + 1) * CH, CH)
                gate_part = dot(w_in_ref[layer, first, :], values, 1, 1) + b_in_ref[layer, first, :]
                value_part = dot(w_in_ref[layer, second, :], values, 1, 1) + b_in_ref[layer, second, :]
                gated = jax.nn.sigmoid(gate_part) * value_part * mask
                wide[half, pl.ds(i, CH, stride=BAND), :] = gated

        rows = band_rows(band)

        @pl.loop(0, CH // 8)
        def _(group):
            channels = pl.ds(pl.multiple_of(group * 8, 8), 8)
            source = pl.ds(pl.multiple_of(group * (8 * BAND), 8 * BAND), 8 * BAND)
            for half in range(2):
                block = wide[half, source, :].astype(jnp.bfloat16).reshape(8, BAND, TILE_J)
                edges_out[layer, channels, half, rows, :] = block

    def send_edges(layer, band):
        rows = band_rows(band)
        place = edges_in.at[layer, :, row, rows, pl.ds(pl.multiple_of(col * TILE_J, TILE_J), TILE_J)]
        sem = edge_recv.at[layer, band]

        @pl.loop(1, DEVICES)
        def _(step):
            to_row, to_col = partner(step, row, col)
            pltpu.make_async_remote_copy(
                src_ref=edges_out.at[layer, to_row * COLS + to_col, :, rows, :],
                dst_ref=place,
                send_sem=edge_send.at[layer],
                recv_sem=sem,
                device_id=(to_row, to_col),
                device_id_type=MESH,
            ).start()

        pltpu.make_async_copy(edges_out.at[layer, me, :, rows, :], place, sem).start()

    def compute_gate(layer):
        @pl.loop(0, TILE_I)
        def _(line):
            pairs = pl.ds(pl.multiple_of(line * TILE_J, TILE_J), TILE_J)
            logits = dot(normed[pairs, :], w_gate_ref[layer], 1, 0) + b_gate_ref[layer]
            gate[pairs, :] = jax.nn.sigmoid(logits)

    def contract(layer):
        for band in range(PHASES):
            whole = edges_in.at[layer, :, :, band_rows(band), :]
            pltpu.make_async_copy(whole, whole, edge_recv.at[layer, band]).wait()

        @pl.loop(0, 16)
        def _(step):
            i, j = step >> 2, step & 3
            if layer == 0:
                left = edges_in[layer, 0, pl.ds(i * 4, 4)].reshape(256, N)
                right = edges_in[layer, 1, pl.ds(j * 4, 4)].reshape(256, N)
                mixed = dot(left, right, 1, 1)
            else:
                left_at = pl.ds(pl.multiple_of(i * 256, 256), 256)
                right_at = pl.ds(pl.multiple_of(j * 256, 256), 256)
                left = edges_in[layer, 0, :, :, left_at].reshape(N, 256)
                right = edges_in[layer, 1, :, :, right_at].reshape(N, 256)
                mixed = dot(left, right, 0, 0)
            mixed = mixed.astype(jnp.bfloat16)
            for a in range(256 // TILE_I):
                for b in range(256 // TILE_J):
                    owner = (i * (256 // TILE_I) + a) * COLS + j * (256 // TILE_J) + b
                    mixed_out[layer, owner] = mixed[
                        a * TILE_I : (a + 1) * TILE_I, b * TILE_J : (b + 1) * TILE_J
                    ]

    def send_mixed(layer, band):
        rows = band_rows(band)
        place = mixed_in.at[layer, me, rows, :]
        sem = mixed_recv.at[layer, band]

        @pl.loop(1, DEVICES)
        def _(step):
            to_row, to_col = partner(step, row, col)
            pltpu.make_async_remote_copy(
                src_ref=mixed_out.at[layer, to_row * COLS + to_col, rows, :],
                dst_ref=place,
                send_sem=mixed_send.at[layer],
                recv_sem=sem,
                device_id=(to_row, to_col),
                device_id_type=MESH,
            ).start()

        pltpu.make_async_copy(mixed_out.at[layer, me, rows, :], place, sem).start()

    def finish(layer, band):
        rows = band_rows(band)
        whole = mixed_in.at[layer, :, rows, :]
        pltpu.make_async_copy(whole, whole, mixed_recv.at[layer, band]).wait()

        @pl.loop(0, CH // 8)
        def _(group):
            channels = pl.ds(pl.multiple_of(group * 8, 8), 8)
            block = mixed_in[layer, channels, rows, :].astype(jnp.float32)
            target = pl.ds(pl.multiple_of(group * (8 * BAND), 8 * BAND), 8 * BAND)
            wide[0, target, :] = block.reshape(8 * BAND, TILE_J)

        @pl.loop(0, BAND)
        def _(i):
            pairs = pl.ds(pl.multiple_of((band * BAND + i) * TILE_J, TILE_J), TILE_J)
            hidden = normalize(
                wide[0, pl.ds(i, CH, stride=BAND), :],
                hidden_gain_ref[layer],
                hidden_shift_ref[layer],
                0,
            ).astype(jnp.bfloat16)
            out = dot(hidden, w_out_ref[layer], 0, 0) + b_out_ref[layer]
            updated = current[pairs, :].astype(jnp.float32) + gate[pairs, :] * out
            current[pairs, :] = updated.astype(jnp.bfloat16)

    @pl.loop(0, PHASES)
    def _(band):
        load(band).wait()
        project(0, band)

        @pl.when(band == 0)
        def _():
            pl.semaphore_wait(barrier, DEVICES - 1)

        send_edges(0, band)

    compute_gate(0)
    contract(0)

    @pl.loop(0, PHASES)
    def _(band):
        send_mixed(0, band)

    @pl.loop(0, PHASES)
    def _(band):
        finish(0, band)
        project(1, band)
        send_edges(1, band)

    compute_gate(1)
    contract(1)

    @pl.loop(0, PHASES)
    def _(band):
        send_mixed(1, band)

    @pl.loop(0, PHASES)
    def _(band):
        finish(1, band)
        store(band).start()

    others = pl.ds(0, DEVICES - 1)
    for layer in range(2):
        sent = edges_out.at[layer, others]
        pltpu.make_async_copy(sent, sent, edge_send.at[layer]).wait()
        sent = mixed_out.at[layer, others]
        pltpu.make_async_copy(sent, sent, mixed_send.at[layer]).wait()
    for band in range(PHASES):
        store(band).wait()


def local(pair, chain_index, norm_gain, norm_shift, w_in, b_in, w_out, b_out):
    valid = (chain_index < NCHAIN - 1).astype(jnp.float32)
    row_valid = lax.dynamic_slice_in_dim(valid, lax.axis_index("row") * TILE_I, TILE_I)
    col_valid = lax.dynamic_slice_in_dim(valid, lax.axis_index("col") * TILE_J, TILE_J)
    mask = row_valid[:, None] * col_valid[None, :]
    weights = jnp.transpose(w_in[:, :, :4], (0, 2, 3, 1)).reshape(2, 4 * CH, CH)
    biases = jnp.broadcast_to(b_in[:, :4].reshape(2, 4 * CH, 1), (2, 4 * CH, TILE_J))
    hidden_gain = jnp.broadcast_to(norm_gain[:, 1, :, None], (2, CH, TILE_J))
    hidden_shift = jnp.broadcast_to(norm_shift[:, 1, :, None], (2, CH, TILE_J))
    operands = (
        pair.reshape(TILE_I * TILE_J, CH),
        mask,
        weights,
        biases,
        w_in[:, :, 4],
        b_in[:, 4:5],
        norm_gain[:, 0:1],
        norm_shift[:, 0:1],
        hidden_gain,
        hidden_shift,
        w_out,
        b_out[:, None],
    )
    vmem = pl.BlockSpec(memory_space=pltpu.VMEM)
    anywhere = pl.BlockSpec(memory_space=pl.ANY)
    pairs = TILE_I * TILE_J
    updated = pl.pallas_call(
        kernel,
        out_shape=jax.ShapeDtypeStruct((pairs, CH), jnp.bfloat16),
        in_specs=[anywhere] + [vmem] * (len(operands) - 1),
        out_specs=anywhere,
        scratch_shapes=[
            pltpu.VMEM((pairs, CH), jnp.bfloat16),
            pltpu.VMEM((pairs, CH), jnp.bfloat16),
            pltpu.VMEM((pairs, CH), jnp.float32),
            pltpu.VMEM((2, CH * BAND, TILE_J), jnp.float32),
            pltpu.VMEM((2, DEVICES, 2, TILE_I, TILE_J), jnp.bfloat16),
            pltpu.VMEM((2, 2, ROWS, TILE_I, N), jnp.bfloat16),
            pltpu.VMEM((2, DEVICES, TILE_I, TILE_J), jnp.bfloat16),
            pltpu.VMEM((2, DEVICES, TILE_I, TILE_J), jnp.bfloat16),
            pltpu.SemaphoreType.DMA((PHASES,)),
            pltpu.SemaphoreType.DMA((2,)),
            pltpu.SemaphoreType.DMA((2, PHASES)),
            pltpu.SemaphoreType.DMA((2,)),
            pltpu.SemaphoreType.DMA((2, PHASES)),
            pltpu.SemaphoreType.DMA((PHASES,)),
        ],
        compiler_params=pltpu.CompilerParams(
            collective_id=1, has_side_effects=True, vmem_limit_bytes=56 << 20
        ),
        name="triangles",
    )(*operands)
    return updated.reshape(TILE_I, TILE_J, CH)


def solution(mesh):
    in_specs = (P("row", "col", None), P(), P(), P(), P(), P(), P(), P())
    out_specs = P("row", "col", None)
    return jax.shard_map(local, mesh=mesh, in_specs=in_specs, out_specs=out_specs, check_vma=False)
```

```python
import jax
import jax.numpy as jnp
from jax import lax
from jax.experimental import pallas as pl
from jax.experimental.pallas import tpu as pltpu
from jax.sharding import PartitionSpec as P

NCHAIN = 4
N = 1024
CH = 128
ROWS = 16
COLS = 8
DEVICES = ROWS * COLS
TILE_I = N // ROWS
TILE_J = N // COLS
PHASES = 4
BAND = TILE_I // PHASES
GROUP = 4
WIDE = GROUP * TILE_J
STRIDE = 31
MESH = pl.DeviceIdType.MESH
EPS = 1e-05


def partner(step, row, col):
    code = (STRIDE * step) & (DEVICES - 1)
    low, mid = code, code >> 2
    x = ((row >> 2) + low) & 3
    y = (col + mid + 2 * low) & 3
    z = (2 * (col >> 2) + ((row >> 1) & 1) + (code >> 4) + 2 * mid) & 3
    core = (row + (code >> 6)) & 1
    return 4 * x + 2 * (z & 1) + core, 4 * (z >> 1) + y


def dot(left, right, left_dim, right_dim):
    return lax.dot_general(
        left, right, (((left_dim,), (right_dim,)), ((), ())), preferred_element_type=jnp.float32
    )


def kernel(
    pair_ref,
    chain_lines_ref,
    chain_ref,
    gain_ref,
    shift_ref,
    w_in_ref,
    b_in_ref,
    w_out_ref,
    b_out_ref,
    out_ref,
    current,
    normed,
    gate,
    wide,
    edges_out,
    edges_in,
    mixed_out,
    mixed_in,
    b_column,
    hidden_column,
    load_sem,
    edge_send,
    edge_recv,
    mixed_send,
    mixed_recv,
    store_sem,
):
    row, col = lax.axis_index("row"), lax.axis_index("col")
    me = row * COLS + col
    barrier = pltpu.get_barrier_semaphore()
    average = jnp.full((CH, CH), 1.0 / CH, jnp.bfloat16)

    def band_rows(band):
        return pl.ds(pl.multiple_of(band * BAND, BAND), BAND)

    def load(band):
        rows = band_rows(band)
        return pltpu.make_async_copy(pair_ref.at[rows], current.at[rows], load_sem.at[band])

    def store(band):
        rows = band_rows(band)
        return pltpu.make_async_copy(current.at[rows], out_ref.at[rows], store_sem.at[band])

    for band in range(PHASES):
        load(band).start()

    @pl.loop(1, DEVICES)
    def _(step):
        pl.semaphore_signal(barrier, inc=1, device_id=partner(step, row, col), device_id_type=MESH)

    def column(values):
        return jnp.transpose(jnp.broadcast_to(values, (CH, CH)))

    for layer in range(2):
        for part in range(4):
            scale = 0.5 if part % 2 == 0 else 1.0
            b_column[layer, part] = column(b_in_ref[layer, part : part + 1, :] * scale)
        hidden_column[layer, 0] = column(gain_ref[layer, 1:2, :])
        hidden_column[layer, 1] = column(shift_ref[layer, 1:2, :])

    def project(layer, band):
        col_half = jnp.where(chain_lines_ref[pl.ds(col, 1), :] < NCHAIN - 1, 0.5, 0.0)

        @pl.loop(0, BAND // GROUP)
        def _(step):
            first = band * BAND + step * GROUP
            lines = pl.ds(first, GROUP)
            values = current[lines].reshape(WIDE, CH)
            centred = values.astype(jnp.float32) - dot(values, average, 1, 0)
            spread = dot(jnp.square(centred).astype(jnp.bfloat16), average, 1, 0)
            values = centred * lax.rsqrt(spread + EPS) * gain_ref[layer, 0:1, :]
            values = (values + shift_ref[layer, 0:1, :]).astype(jnp.bfloat16)
            normed[lines] = values.reshape(GROUP, TILE_J, CH)
            masks = []
            for i in range(GROUP):
                chain = chain_ref[row * TILE_I + first + i]
                masks.append(col_half * jnp.where(chain < NCHAIN - 1, 1.0, 0.0))
            for half in range(2):
                opening = dot(w_in_ref[layer, 2 * half], values, 1, 1)
                content = dot(w_in_ref[layer, 2 * half + 1], values, 1, 1)
                for i in range(GROUP):
                    at = slice(i * TILE_J, (i + 1) * TILE_J)
                    factor = jnp.tanh(opening[:, at] + b_column[layer, 2 * half]) + 1.0
                    gated = factor * (content[:, at] + b_column[layer, 2 * half + 1]) * masks[i]
                    wide[half, pl.ds(step * GROUP + i, CH, stride=BAND), :] = gated

        rows = band_rows(band)

        @pl.loop(0, CH // 32)
        def _(group):
            channels = pl.ds(pl.multiple_of(group * 32, 32), 32)
            source = pl.ds(pl.multiple_of(group * (32 * BAND), 32 * BAND), 32 * BAND)
            for half in range(2):
                block = wide[half, source, :].astype(jnp.bfloat16).reshape(32, BAND, TILE_J)
                edges_out[layer, channels, half, rows, :] = block

    def send_edges(layer, band):
        rows = band_rows(band)
        place = edges_in.at[layer, :, row, rows, pl.ds(pl.multiple_of(col * TILE_J, TILE_J), TILE_J)]
        sem = edge_recv.at[layer, band]

        @pl.loop(1, DEVICES)
        def _(step):
            to_row, to_col = partner(step, row, col)
            pltpu.make_async_remote_copy(
                src_ref=edges_out.at[layer, to_row * COLS + to_col, :, rows, :],
                dst_ref=place,
                send_sem=edge_send.at[layer],
                recv_sem=sem,
                device_id=(to_row, to_col),
                device_id_type=MESH,
            ).start()

        pltpu.make_async_copy(edges_out.at[layer, me, :, rows, :], place, sem).start()

    def compute_gate(layer):
        @pl.loop(0, TILE_I // GROUP)
        def _(step):
            lines = pl.ds(step * GROUP, GROUP)
            logits = dot(normed[lines].reshape(WIDE, CH), w_in_ref[layer, 4], 1, 1)
            half = 0.5 * jnp.tanh(logits + 0.5 * b_in_ref[layer, 4:5, :]) + 0.5
            gate[lines] = half.reshape(GROUP, TILE_J, CH)

    def contract(layer):
        for band in range(PHASES):
            whole = edges_in.at[layer, :, :, band_rows(band), :]
            pltpu.make_async_copy(whole, whole, edge_recv.at[layer, band]).wait()

        @pl.loop(0, 16)
        def _(step):
            i, j = step >> 2, step & 3
            if layer == 0:
                left = edges_in[layer, 0, pl.ds(i * 4, 4)].reshape(256, N)
                right = edges_in[layer, 1, pl.ds(j * 4, 4)].reshape(256, N)
                mixed = dot(left, right, 1, 1)
            else:
                left_at = pl.ds(pl.multiple_of(i * 256, 256), 256)
                right_at = pl.ds(pl.multiple_of(j * 256, 256), 256)
                left = edges_in[layer, 0, :, :, left_at].reshape(N, 256)
                right = edges_in[layer, 1, :, :, right_at].reshape(N, 256)
                mixed = dot(left, right, 0, 0)
            mixed = mixed.astype(jnp.bfloat16)
            for a in range(256 // TILE_I):
                for b in range(256 // TILE_J):
                    owner = (i * (256 // TILE_I) + a) * COLS + j * (256 // TILE_J) + b
                    mixed_out[layer, owner] = mixed[
                        a * TILE_I : (a + 1) * TILE_I, b * TILE_J : (b + 1) * TILE_J
                    ]

    def send_mixed(layer, band):
        rows = band_rows(band)
        place = mixed_in.at[layer, me, rows, :]
        sem = mixed_recv.at[layer, band]

        @pl.loop(1, DEVICES)
        def _(step):
            to_row, to_col = partner(step, row, col)
            pltpu.make_async_remote_copy(
                src_ref=mixed_out.at[layer, to_row * COLS + to_col, rows, :],
                dst_ref=place,
                send_sem=mixed_send.at[layer],
                recv_sem=sem,
                device_id=(to_row, to_col),
                device_id_type=MESH,
            ).start()

        pltpu.make_async_copy(mixed_out.at[layer, me, rows, :], place, sem).start()

    def finish(layer, band):
        rows = band_rows(band)
        whole = mixed_in.at[layer, :, rows, :]
        pltpu.make_async_copy(whole, whole, mixed_recv.at[layer, band]).wait()

        @pl.loop(0, CH // 32)
        def _(group):
            channels = pl.ds(pl.multiple_of(group * 32, 32), 32)
            block = mixed_in[layer, channels, rows, :].astype(jnp.float32)
            target = pl.ds(pl.multiple_of(group * (32 * BAND), 32 * BAND), 32 * BAND)
            wide[0, target, :] = block.reshape(32 * BAND, TILE_J)

        @pl.loop(0, BAND // GROUP)
        def _(step):
            for i in range(GROUP):
                line = band * BAND + step * GROUP + i
                values = wide[0, pl.ds(step * GROUP + i, CH, stride=BAND), :]
                centred = values - jnp.mean(values, axis=0, keepdims=True)
                spread = jnp.mean(jnp.square(centred), axis=0, keepdims=True)
                hidden = centred * lax.rsqrt(spread + EPS) * hidden_column[layer, 0]
                hidden = (hidden + hidden_column[layer, 1]).astype(jnp.bfloat16)
                out = dot(hidden, w_out_ref[layer], 0, 0) + b_out_ref[layer : layer + 1, :]
                updated = current[line].astype(jnp.float32) + gate[line] * out
                current[line] = updated.astype(jnp.bfloat16)

    @pl.loop(0, PHASES)
    def _(band):
        load(band).wait()
        project(0, band)

        @pl.when(band == 0)
        def _():
            pl.semaphore_wait(barrier, DEVICES - 1)

        send_edges(0, band)

    compute_gate(0)
    contract(0)

    @pl.loop(0, PHASES)
    def _(band):
        send_mixed(0, band)

    @pl.loop(0, PHASES)
    def _(band):
        finish(0, band)
        project(1, band)
        send_edges(1, band)

    compute_gate(1)
    contract(1)

    @pl.loop(0, PHASES)
    def _(band):
        send_mixed(1, band)

    @pl.loop(0, PHASES)
    def _(band):
        finish(1, band)
        store(band).start()

    others = pl.ds(0, DEVICES - 1)
    for layer in range(2):
        sent = edges_out.at[layer, others]
        pltpu.make_async_copy(sent, sent, edge_send.at[layer]).wait()
        sent = mixed_out.at[layer, others]
        pltpu.make_async_copy(sent, sent, mixed_send.at[layer]).wait()
    for band in range(PHASES):
        store(band).wait()


def local(pair, chain_index, norm_gain, norm_shift, w_in, b_in, w_out, b_out):
    halves = jnp.array([0.5, 1.0, 0.5, 1.0, 0.5], jnp.bfloat16)
    weights = jnp.transpose(w_in, (0, 2, 3, 1)) * halves[None, :, None, None]
    vmem = pl.BlockSpec(memory_space=pltpu.VMEM)
    smem = pl.BlockSpec(memory_space=pltpu.SMEM)
    anywhere = pl.BlockSpec(memory_space=pl.ANY)
    tile = (TILE_I, TILE_J, CH)
    return pl.pallas_call(
        kernel,
        out_shape=jax.ShapeDtypeStruct(tile, jnp.bfloat16),
        in_specs=[anywhere, vmem, smem] + [vmem] * 6,
        out_specs=anywhere,
        scratch_shapes=[
            pltpu.VMEM(tile, jnp.bfloat16),
            pltpu.VMEM(tile, jnp.bfloat16),
            pltpu.VMEM(tile, jnp.float32),
            pltpu.VMEM((2, CH * BAND, TILE_J), jnp.float32),
            pltpu.VMEM((2, DEVICES, 2, TILE_I, TILE_J), jnp.bfloat16),
            pltpu.VMEM((2, 2, ROWS, TILE_I, N), jnp.bfloat16),
            pltpu.VMEM((2, DEVICES, TILE_I, TILE_J), jnp.bfloat16),
            pltpu.VMEM((2, DEVICES, TILE_I, TILE_J), jnp.bfloat16),
            pltpu.VMEM((2, 4, CH, TILE_J), jnp.float32),
            pltpu.VMEM((2, 2, CH, TILE_J), jnp.float32),
            pltpu.SemaphoreType.DMA((PHASES,)),
            pltpu.SemaphoreType.DMA((2,)),
            pltpu.SemaphoreType.DMA((2, PHASES)),
            pltpu.SemaphoreType.DMA((2,)),
            pltpu.SemaphoreType.DMA((2, PHASES)),
            pltpu.SemaphoreType.DMA((PHASES,)),
        ],
        compiler_params=pltpu.CompilerParams(
            collective_id=1, has_side_effects=True, vmem_limit_bytes=56 << 20
        ),
        name="triangles",
    )(
        pair,
        chain_index.reshape(COLS, TILE_J),
        chain_index,
        norm_gain,
        norm_shift,
        weights,
        b_in,
        w_out,
        b_out,
    )


def solution(mesh):
    in_specs = (P("row", "col", None), P(), P(), P(), P(), P(), P(), P())
    out_specs = P("row", "col", None)
    return jax.shard_map(local, mesh=mesh, in_specs=in_specs, out_specs=out_specs, check_vma=False)
```

```python
import jax
import jax.numpy as jnp
from jax import lax
from jax.experimental import pallas as pl
from jax.experimental.pallas import tpu as pltpu
from jax.sharding import PartitionSpec as P

NCHAIN = 4
N = 1024
CH = 128
ROWS = 16
COLS = 8
DEVICES = ROWS * COLS
TILE_I = N // ROWS
TILE_J = N // COLS
PHASES = 4
BAND = TILE_I // PHASES
GROUP = 4
WIDE = GROUP * TILE_J
STRIDE = 31
MESH = pl.DeviceIdType.MESH
EPS = 1e-05


def partner(step, row, col):
    code = (STRIDE * step) & (DEVICES - 1)
    low, mid = code, code >> 2
    x = ((row >> 2) + low) & 3
    y = (col + mid + 2 * low) & 3
    z = (2 * (col >> 2) + ((row >> 1) & 1) + (code >> 4) + 2 * mid) & 3
    core = (row + (code >> 6)) & 1
    return 4 * x + 2 * (z & 1) + core, 4 * (z >> 1) + y


def dot(left, right, left_dim, right_dim):
    return lax.dot_general(
        left, right, (((left_dim,), (right_dim,)), ((), ())), preferred_element_type=jnp.float32
    )


def kernel(
    pair_ref,
    chain_lines_ref,
    chain_ref,
    gain_ref,
    shift_ref,
    w_in_ref,
    b_in_ref,
    w_out_ref,
    b_out_ref,
    out_ref,
    current,
    normed,
    gate,
    wide,
    edges_out,
    edges_in,
    mixed_out,
    mixed_in,
    partial,
    weights,
    b_column,
    hidden_column,
    load_sem,
    edge_send,
    edge_recv,
    mixed_send,
    mixed_recv,
    store_sem,
    ready_sem,
):
    row, col = lax.axis_index("row"), lax.axis_index("col")
    me = row * COLS + col
    barrier = pltpu.get_barrier_semaphore()
    average = jnp.full((CH, CH), 1.0 / CH, jnp.bfloat16)

    def band_rows(band):
        return pl.ds(pl.multiple_of(band * BAND, BAND), BAND)

    def load(band):
        rows = band_rows(band)
        return pltpu.make_async_copy(pair_ref.at[rows], current.at[rows], load_sem.at[band])

    def store(band):
        rows = band_rows(band)
        return pltpu.make_async_copy(current.at[rows], out_ref.at[rows], store_sem.at[band])

    for band in range(PHASES):
        load(band).start()

    def greet(sem, length, device):
        @pl.loop(1, length)
        def _(step):
            pl.semaphore_signal(sem, inc=1, device_id=device(step), device_id_type=MESH)

    greet(barrier, ROWS, lambda step: ((row + step) & (ROWS - 1), col))
    greet(barrier, COLS, lambda step: (row, (col + step) & (COLS - 1)))

    def column(values):
        return jnp.transpose(jnp.broadcast_to(values, (CH, CH)))

    for layer in range(2):
        for part in range(4):
            scale = 0.5 if part % 2 == 0 else 1.0
            b_column[layer, part] = column(b_in_ref[part, layer : layer + 1, :] * scale)
        for part in range(5):
            scale = 0.5 if part % 2 == 0 else 1.0
            turned = jnp.transpose(w_in_ref[layer, part].astype(jnp.float32)) * scale
            weights[layer, part] = turned.astype(jnp.bfloat16)
        hidden_column[layer, 0] = column(gain_ref[layer, 1:2, :])
        hidden_column[layer, 1] = column(shift_ref[layer, 1:2, :])

    def project(layer, band, halves, norm):
        col_half = jnp.where(chain_lines_ref[pl.ds(col, 1), :] < NCHAIN - 1, 0.5, 0.0)

        @pl.loop(0, BAND // GROUP)
        def _(step):
            first = band * BAND + step * GROUP
            lines = pl.ds(first, GROUP)
            if norm:
                values = current[lines].reshape(WIDE, CH)
                centred = values.astype(jnp.float32) - dot(values, average, 1, 0)
                spread = dot(jnp.square(centred).astype(jnp.bfloat16), average, 1, 0)
                values = centred * lax.rsqrt(spread + EPS) * gain_ref[layer, 0:1, :]
                values = (values + shift_ref[layer, 0:1, :]).astype(jnp.bfloat16)
                normed[lines] = values.reshape(GROUP, TILE_J, CH)
            else:
                values = normed[lines].reshape(WIDE, CH)
            masks = []
            for i in range(GROUP):
                chain = chain_ref[row * TILE_I + first + i]
                masks.append(col_half * jnp.where(chain < NCHAIN - 1, 1.0, 0.0))
            for half in halves:
                opening = dot(weights[layer, 2 * half], values, 1, 1)
                content = dot(weights[layer, 2 * half + 1], values, 1, 1)
                for i in range(GROUP):
                    at = slice(i * TILE_J, (i + 1) * TILE_J)
                    factor = jnp.tanh(opening[:, at] + b_column[layer, 2 * half]) + 1.0
                    gated = factor * (content[:, at] + b_column[layer, 2 * half + 1]) * masks[i]
                    wide[half, pl.ds(step * GROUP + i, CH, stride=BAND), :] = gated

        rows = band_rows(band)

        @pl.loop(0, CH // 32)
        def _(group):
            channels = pl.ds(pl.multiple_of(group * 32, 32), 32)
            source = pl.ds(pl.multiple_of(group * (32 * BAND), 32 * BAND), 32 * BAND)
            for half in halves:
                block = wide[half, source, :].astype(jnp.bfloat16).reshape(32, BAND, TILE_J)
                edges_out[channels, half, rows, :] = block

    def send_edges(layer, band, half):
        rows = band_rows(band)
        halves = slice(None) if half is None else half
        sem = edge_recv.at[layer, half or 0, band]
        place = edges_in.at[
            layer, halves, row, rows, pl.ds(pl.multiple_of(col * TILE_J, TILE_J), TILE_J)
        ]

        @pl.loop(1, DEVICES)
        def _(step):
            to_row, to_col = partner(step, row, col)
            pltpu.make_async_remote_copy(
                src_ref=edges_out.at[to_row * COLS + to_col, halves, rows, :],
                dst_ref=place,
                send_sem=edge_send.at[layer],
                recv_sem=sem,
                device_id=(to_row, to_col),
                device_id_type=MESH,
            ).start()

        pltpu.make_async_copy(edges_out.at[me, halves, rows, :], place, sem).start()

    def wait_edges(layer, band, half):
        halves = slice(None) if half is None else half
        whole = edges_in.at[layer, halves, :, band_rows(band), :]
        pltpu.make_async_copy(whole, whole, edge_recv.at[layer, half or 0, band]).wait()

    def wait_sent(buffer, sem):
        sent = buffer.at[pl.ds(0, DEVICES - 1)]
        pltpu.make_async_copy(sent, sent, sem).wait()

    def compute_gate(layer):
        @pl.loop(0, TILE_I // GROUP)
        def _(step):
            lines = pl.ds(step * GROUP, GROUP)
            logits = dot(normed[lines].reshape(WIDE, CH), weights[layer, 4], 1, 1)
            half = 0.5 * jnp.tanh(logits + 0.5 * b_in_ref[4, layer : layer + 1, :]) + 0.5
            gate[lines] = half.reshape(GROUP, TILE_J, CH)

    def contract_rows(band):
        rows = band_rows(band)
        left = edges_in[0, 0, :, rows, :].reshape(ROWS * BAND, N)

        @pl.loop(0, N // 256)
        def _(j):
            right = edges_in[0, 1, pl.ds(j * (256 // TILE_I), 256 // TILE_I)].reshape(256, N)
            mixed = dot(left, right, 1, 1).astype(jnp.bfloat16).reshape(ROWS, BAND, 256)
            for b in range(256 // TILE_J):
                lanes = slice(b * TILE_J, (b + 1) * TILE_J)
                for r in range(ROWS):
                    owner = r * COLS + j * (256 // TILE_J) + b
                    mixed_out[owner, rows, :] = mixed[r, :, lanes]

    def contract_columns(first, last):
        rows = slice(first * BAND, last * BAND)
        depth = ROWS * (last - first) * BAND

        @pl.loop(0, N // 256)
        def _(i):
            lanes = pl.ds(pl.multiple_of(i * 256, 256), 256)
            left = edges_in[1, 0, :, rows, lanes].reshape(depth, 256)
            for j in range(N // 256):
                right = edges_in[1, 1, :, rows, j * 256 : (j + 1) * 256].reshape(depth, 256)
                mixed = dot(left, right, 0, 0)
                if first:
                    mixed = mixed + partial[i, j]
                if last < PHASES:
                    partial[i, j] = mixed
                    continue
                mixed = mixed.astype(jnp.bfloat16)
                for a in range(256 // TILE_I):
                    for b in range(256 // TILE_J):
                        owner = (i * (256 // TILE_I) + a) * COLS + j * (256 // TILE_J) + b
                        mixed_out[owner] = mixed[
                            a * TILE_I : (a + 1) * TILE_I, b * TILE_J : (b + 1) * TILE_J
                        ]

    def send_mixed(layer, band):
        rows = band_rows(band)
        place = mixed_in.at[layer, me, rows, :]
        sem = mixed_recv.at[layer, band]

        @pl.loop(1, DEVICES)
        def _(step):
            to_row, to_col = partner(step, row, col)
            pltpu.make_async_remote_copy(
                src_ref=mixed_out.at[to_row * COLS + to_col, rows, :],
                dst_ref=place,
                send_sem=mixed_send.at[layer],
                recv_sem=sem,
                device_id=(to_row, to_col),
                device_id_type=MESH,
            ).start()

        pltpu.make_async_copy(mixed_out.at[me, rows, :], place, sem).start()

    def finish(layer, band):
        rows = band_rows(band)
        whole = mixed_in.at[layer, :, rows, :]
        pltpu.make_async_copy(whole, whole, mixed_recv.at[layer, band]).wait()

        @pl.loop(0, CH // 32)
        def _(group):
            channels = pl.ds(pl.multiple_of(group * 32, 32), 32)
            block = mixed_in[layer, channels, rows, :].astype(jnp.float32)
            target = pl.ds(pl.multiple_of(group * (32 * BAND), 32 * BAND), 32 * BAND)
            wide[0, target, :] = block.reshape(32 * BAND, TILE_J)

        @pl.loop(0, BAND // GROUP)
        def _(step):
            for i in range(GROUP):
                line = band * BAND + step * GROUP + i
                values = wide[0, pl.ds(step * GROUP + i, CH, stride=BAND), :]
                centred = values - jnp.mean(values, axis=0, keepdims=True)
                spread = jnp.mean(jnp.square(centred), axis=0, keepdims=True)
                hidden = centred * lax.rsqrt(spread + EPS) * hidden_column[layer, 0]
                hidden = (hidden + hidden_column[layer, 1]).astype(jnp.bfloat16)
                out = dot(hidden, w_out_ref[layer], 0, 0) + b_out_ref[layer : layer + 1, :]
                updated = current[line].astype(jnp.float32) + gate[line] * out
                current[line] = updated.astype(jnp.bfloat16)

    pl.semaphore_wait(barrier, ROWS - 1 + COLS - 1)
    greet(ready_sem, COLS, lambda step: (row, (col + step) & (COLS - 1)))

    @pl.loop(0, PHASES)
    def _(band):
        load(band).wait()
        project(0, band, (1,), True)

        @pl.when(band == 0)
        def _():
            pl.semaphore_wait(ready_sem, COLS - 1)

        send_edges(0, band, 1)

    @pl.loop(0, PHASES)
    def _(band):
        project(0, band, (0,), False)
        send_edges(0, band, 0)

    compute_gate(0)
    for band in range(PHASES):
        wait_edges(0, band, 1)

    @pl.loop(0, PHASES)
    def _(band):
        wait_edges(0, band, 0)
        contract_rows(band)
        send_mixed(0, band)

    wait_sent(edges_out, edge_send.at[0])

    @pl.loop(0, PHASES)
    def _(band):
        finish(0, band)
        project(1, band, (0, 1), True)
        send_edges(1, band, None)

    compute_gate(1)
    wait_sent(mixed_out, mixed_send.at[0])
    for band in range(PHASES - 1):
        wait_edges(1, band, None)
    contract_columns(0, PHASES - 1)
    wait_edges(1, PHASES - 1, None)
    contract_columns(PHASES - 1, PHASES)

    @pl.loop(0, PHASES)
    def _(band):
        send_mixed(1, band)

    @pl.loop(0, PHASES)
    def _(band):
        finish(1, band)
        store(band).start()

    wait_sent(edges_out, edge_send.at[1])
    wait_sent(mixed_out, mixed_send.at[1])
    for band in range(PHASES):
        store(band).wait()


def local(pair, chain_index, norm_gain, norm_shift, w_in, b_in, w_out, b_out):
    weights = jnp.transpose(w_in, (0, 2, 1, 3))
    biases = jnp.transpose(b_in, (1, 0, 2))
    vmem = pl.BlockSpec(memory_space=pltpu.VMEM)
    smem = pl.BlockSpec(memory_space=pltpu.SMEM)
    anywhere = pl.BlockSpec(memory_space=pl.ANY)
    tile = (TILE_I, TILE_J, CH)
    return pl.pallas_call(
        kernel,
        out_shape=jax.ShapeDtypeStruct(tile, jnp.bfloat16),
        in_specs=[anywhere, vmem, smem] + [vmem] * 6,
        out_specs=anywhere,
        scratch_shapes=[
            pltpu.VMEM(tile, jnp.bfloat16),
            pltpu.VMEM(tile, jnp.bfloat16),
            pltpu.VMEM(tile, jnp.float32),
            pltpu.VMEM((2, CH * BAND, TILE_J), jnp.float32),
            pltpu.VMEM((DEVICES, 2, TILE_I, TILE_J), jnp.bfloat16),
            pltpu.VMEM((2, 2, ROWS, TILE_I, N), jnp.bfloat16),
            pltpu.VMEM((DEVICES, TILE_I, TILE_J), jnp.bfloat16),
            pltpu.VMEM((2, DEVICES, TILE_I, TILE_J), jnp.bfloat16),
            pltpu.VMEM((N // 256, N // 256, 256, 256), jnp.float32),
            pltpu.VMEM((2, 5, CH, CH), jnp.bfloat16),
            pltpu.VMEM((2, 4, CH, TILE_J), jnp.float32),
            pltpu.VMEM((2, 2, CH, TILE_J), jnp.float32),
            pltpu.SemaphoreType.DMA((PHASES,)),
            pltpu.SemaphoreType.DMA((2,)),
            pltpu.SemaphoreType.DMA((2, 2, PHASES)),
            pltpu.SemaphoreType.DMA((2,)),
            pltpu.SemaphoreType.DMA((2, PHASES)),
            pltpu.SemaphoreType.DMA((PHASES,)),
            pltpu.SemaphoreType.REGULAR,
        ],
        compiler_params=pltpu.CompilerParams(
            collective_id=1, has_side_effects=True, vmem_limit_bytes=56 << 20
        ),
        name="triangles",
    )(
        pair,
        chain_index.reshape(COLS, TILE_J),
        chain_index,
        norm_gain,
        norm_shift,
        weights,
        biases,
        w_out,
        b_out,
    )


def solution(mesh):
    in_specs = (P("row", "col", None), P(), P(), P(), P(), P(), P(), P())
    out_specs = P("row", "col", None)
    return jax.shard_map(local, mesh=mesh, in_specs=in_specs, out_specs=out_specs, check_vma=False)
```

```python
import jax
import jax.numpy as jnp
from jax import lax
from jax.experimental import pallas as pl
from jax.experimental.pallas import tpu as pltpu
from jax.sharding import PartitionSpec as P

NCHAIN = 4
N = 1024
CH = 128
ROWS = 16
COLS = 8
DEVICES = ROWS * COLS
TILE_I = N // ROWS
TILE_J = N // COLS
PHASES = 4
BAND = TILE_I // PHASES
GROUP = 4
WIDE = GROUP * TILE_J
STRIDE = 97
MESH = pl.DeviceIdType.MESH
EPS = 1e-05


def partner(step, row, col):
    code = (STRIDE * step) & (DEVICES - 1)
    low, mid = code, code >> 2
    x = ((row >> 2) + low) & 3
    y = (col + mid + 2 * low) & 3
    z = (2 * (col >> 2) + ((row >> 1) & 1) + (code >> 4) + 2 * mid) & 3
    core = (row + (code >> 6)) & 1
    return 4 * x + 2 * (z & 1) + core, 4 * (z >> 1) + y


def dot(left, right, left_dim, right_dim):
    return lax.dot_general(
        left, right, (((left_dim,), (right_dim,)), ((), ())), preferred_element_type=jnp.float32
    )


def kernel(
    pair_ref,
    chain_lines_ref,
    chain_ref,
    gain_ref,
    shift_ref,
    w_in_ref,
    b_in_ref,
    w_out_ref,
    b_out_ref,
    out_ref,
    current,
    normed,
    gate,
    wide,
    edges_out,
    edges_in,
    mixed_out,
    mixed_in,
    partial,
    weights,
    b_column,
    hidden_column,
    load_sem,
    edge_send,
    edge_recv,
    mixed_send,
    mixed_recv,
    store_sem,
    ready_sem,
):
    row, col = lax.axis_index("row"), lax.axis_index("col")
    me = row * COLS + col
    barrier = pltpu.get_barrier_semaphore()
    average = jnp.full((CH, CH), 1.0 / CH, jnp.bfloat16)

    def band_rows(band):
        return pl.ds(pl.multiple_of(band * BAND, BAND), BAND)

    def load(band):
        rows = band_rows(band)
        return pltpu.make_async_copy(pair_ref.at[rows], current.at[rows], load_sem.at[band])

    def store(band):
        rows = band_rows(band)
        return pltpu.make_async_copy(current.at[rows], out_ref.at[rows], store_sem.at[band])

    for band in range(PHASES):
        load(band).start()

    def greet(sem, length, device):
        @pl.loop(1, length)
        def _(step):
            pl.semaphore_signal(sem, inc=1, device_id=device(step), device_id_type=MESH)

    greet(barrier, ROWS, lambda step: ((row + step) & (ROWS - 1), col))
    greet(barrier, COLS, lambda step: (row, (col + step) & (COLS - 1)))

    def column(values):
        return jnp.transpose(jnp.broadcast_to(values, (CH, CH)))

    for layer in range(2):
        for part in range(4):
            scale = 0.5 if part % 2 == 0 else 1.0
            b_column[layer, part] = column(b_in_ref[part, layer : layer + 1, :] * scale)
        for part in range(5):
            scale = 0.5 if part % 2 == 0 else 1.0
            turned = jnp.transpose(w_in_ref[layer, part].astype(jnp.float32)) * scale
            weights[layer, part] = turned.astype(jnp.bfloat16)
        hidden_column[layer, 0] = column(gain_ref[layer, 1:2, :])
        hidden_column[layer, 1] = column(shift_ref[layer, 1:2, :])

    def project(layer, band, halves, norm):
        col_half = jnp.where(chain_lines_ref[pl.ds(col, 1), :] < NCHAIN - 1, 0.5, 0.0)

        @pl.loop(0, BAND // GROUP)
        def _(step):
            first = band * BAND + step * GROUP
            lines = pl.ds(first, GROUP)
            if norm:
                values = current[lines].reshape(WIDE, CH)
                centred = values.astype(jnp.float32) - dot(values, average, 1, 0)
                spread = dot(jnp.square(centred).astype(jnp.bfloat16), average, 1, 0)
                values = centred * lax.rsqrt(spread + EPS) * gain_ref[layer, 0:1, :]
                values = (values + shift_ref[layer, 0:1, :]).astype(jnp.bfloat16)
                normed[lines] = values.reshape(GROUP, TILE_J, CH)
            else:
                values = normed[lines].reshape(WIDE, CH)
            masks = []
            for i in range(GROUP):
                chain = chain_ref[row * TILE_I + first + i]
                masks.append(col_half * jnp.where(chain < NCHAIN - 1, 1.0, 0.0))
            for half in halves:
                opening = dot(weights[layer, 2 * half], values, 1, 1)
                content = dot(weights[layer, 2 * half + 1], values, 1, 1)
                for i in range(GROUP):
                    at = slice(i * TILE_J, (i + 1) * TILE_J)
                    factor = jnp.tanh(opening[:, at] + b_column[layer, 2 * half]) + 1.0
                    gated = factor * (content[:, at] + b_column[layer, 2 * half + 1]) * masks[i]
                    wide[half, pl.ds(step * GROUP + i, CH, stride=BAND), :] = gated

        rows = band_rows(band)

        @pl.loop(0, CH // 32)
        def _(group):
            channels = pl.ds(pl.multiple_of(group * 32, 32), 32)
            source = pl.ds(pl.multiple_of(group * (32 * BAND), 32 * BAND), 32 * BAND)
            for half in halves:
                block = wide[half, source, :].astype(jnp.bfloat16).reshape(32, BAND, TILE_J)
                edges_out[channels, half, rows, :] = block

    def send_edges(layer, band, half):
        rows = band_rows(band)
        halves = slice(None) if half is None else half
        sem = edge_recv.at[layer, half or 0, band]
        place = edges_in.at[
            layer, halves, row, rows, pl.ds(pl.multiple_of(col * TILE_J, TILE_J), TILE_J)
        ]

        @pl.loop(1, DEVICES)
        def _(step):
            to_row, to_col = partner(step, row, col)
            pltpu.make_async_remote_copy(
                src_ref=edges_out.at[to_row * COLS + to_col, halves, rows, :],
                dst_ref=place,
                send_sem=edge_send.at[layer],
                recv_sem=sem,
                device_id=(to_row, to_col),
                device_id_type=MESH,
            ).start()

        pltpu.make_async_copy(edges_out.at[me, halves, rows, :], place, sem).start()

    def wait_edges(layer, band, half):
        halves = slice(None) if half is None else half
        whole = edges_in.at[layer, halves, :, band_rows(band), :]
        pltpu.make_async_copy(whole, whole, edge_recv.at[layer, half or 0, band]).wait()

    def wait_sent(buffer, sem):
        sent = buffer.at[pl.ds(0, DEVICES - 1)]
        pltpu.make_async_copy(sent, sent, sem).wait()

    def compute_gate(layer):
        @pl.loop(0, TILE_I // GROUP)
        def _(step):
            lines = pl.ds(step * GROUP, GROUP)
            logits = dot(normed[lines].reshape(WIDE, CH), weights[layer, 4], 1, 1)
            half = 0.5 * jnp.tanh(logits + 0.5 * b_in_ref[4, layer : layer + 1, :]) + 0.5
            gate[lines] = half.reshape(GROUP, TILE_J, CH)

    def contract_rows(band):
        rows = band_rows(band)
        left = edges_in[0, 0, :, rows, :].reshape(ROWS * BAND, N)

        @pl.loop(0, N // 256)
        def _(j):
            right = edges_in[0, 1, pl.ds(j * (256 // TILE_I), 256 // TILE_I)].reshape(256, N)
            mixed = dot(left, right, 1, 1).astype(jnp.bfloat16).reshape(ROWS, BAND, 256)
            for b in range(256 // TILE_J):
                lanes = slice(b * TILE_J, (b + 1) * TILE_J)
                for r in range(ROWS):
                    owner = r * COLS + j * (256 // TILE_J) + b
                    mixed_out[owner, rows, :] = mixed[r, :, lanes]

    def contract_columns(first, last):
        rows = slice(first * BAND, last * BAND)
        depth = ROWS * (last - first) * BAND

        @pl.loop(0, N // 256)
        def _(i):
            lanes = pl.ds(pl.multiple_of(i * 256, 256), 256)
            left = edges_in[1, 0, :, rows, lanes].reshape(depth, 256)
            for j in range(N // 256):
                right = edges_in[1, 1, :, rows, j * 256 : (j + 1) * 256].reshape(depth, 256)
                mixed = dot(left, right, 0, 0)
                if first:
                    mixed = mixed + partial[i, j]
                if last < PHASES:
                    partial[i, j] = mixed
                    continue
                mixed = mixed.astype(jnp.bfloat16)
                for a in range(256 // TILE_I):
                    for b in range(256 // TILE_J):
                        owner = (i * (256 // TILE_I) + a) * COLS + j * (256 // TILE_J) + b
                        mixed_out[owner] = mixed[
                            a * TILE_I : (a + 1) * TILE_I, b * TILE_J : (b + 1) * TILE_J
                        ]

    def send_mixed(layer, band):
        rows = band_rows(band)
        place = mixed_in.at[layer, me, rows, :]
        sem = mixed_recv.at[layer, band]

        @pl.loop(1, DEVICES)
        def _(step):
            to_row, to_col = partner(step, row, col)
            pltpu.make_async_remote_copy(
                src_ref=mixed_out.at[to_row * COLS + to_col, rows, :],
                dst_ref=place,
                send_sem=mixed_send.at[layer],
                recv_sem=sem,
                device_id=(to_row, to_col),
                device_id_type=MESH,
            ).start()

        pltpu.make_async_copy(mixed_out.at[me, rows, :], place, sem).start()

    def finish(layer, band):
        rows = band_rows(band)
        whole = mixed_in.at[layer, :, rows, :]
        pltpu.make_async_copy(whole, whole, mixed_recv.at[layer, band]).wait()

        @pl.loop(0, CH // 32)
        def _(group):
            channels = pl.ds(pl.multiple_of(group * 32, 32), 32)
            block = mixed_in[layer, channels, rows, :].astype(jnp.float32)
            target = pl.ds(pl.multiple_of(group * (32 * BAND), 32 * BAND), 32 * BAND)
            wide[0, target, :] = block.reshape(32 * BAND, TILE_J)

        @pl.loop(0, BAND // GROUP)
        def _(step):
            for i in range(GROUP):
                line = band * BAND + step * GROUP + i
                values = wide[0, pl.ds(step * GROUP + i, CH, stride=BAND), :]
                centred = values - jnp.mean(values, axis=0, keepdims=True)
                spread = jnp.mean(jnp.square(centred), axis=0, keepdims=True)
                hidden = centred * lax.rsqrt(spread + EPS) * hidden_column[layer, 0]
                hidden = (hidden + hidden_column[layer, 1]).astype(jnp.bfloat16)
                out = dot(hidden, w_out_ref[layer], 0, 0) + b_out_ref[layer : layer + 1, :]
                updated = current[line].astype(jnp.float32) + gate[line] * out
                current[line] = updated.astype(jnp.bfloat16)

    pl.semaphore_wait(barrier, ROWS - 1 + COLS - 1)
    greet(ready_sem, COLS, lambda step: (row, (col + step) & (COLS - 1)))

    @pl.loop(0, PHASES)
    def _(band):
        load(band).wait()
        project(0, band, (1,), True)

        @pl.when(band == 0)
        def _():
            pl.semaphore_wait(ready_sem, COLS - 1)

        send_edges(0, band, 1)

    @pl.loop(0, PHASES)
    def _(band):
        project(0, band, (0,), False)
        send_edges(0, band, 0)

    compute_gate(0)
    for band in range(PHASES):
        wait_edges(0, band, 1)

    @pl.loop(0, PHASES)
    def _(band):
        wait_edges(0, band, 0)
        contract_rows(band)
        send_mixed(0, band)

    wait_sent(edges_out, edge_send.at[0])

    @pl.loop(0, PHASES)
    def _(band):
        finish(0, band)
        project(1, band, (0, 1), True)
        send_edges(1, band, None)

    compute_gate(1)
    wait_sent(mixed_out, mixed_send.at[0])
    for band in range(PHASES - 1):
        wait_edges(1, band, None)
    contract_columns(0, PHASES - 1)
    wait_edges(1, PHASES - 1, None)
    contract_columns(PHASES - 1, PHASES)

    @pl.loop(0, PHASES)
    def _(band):
        send_mixed(1, band)

    @pl.loop(0, PHASES)
    def _(band):
        finish(1, band)
        store(band).start()

    wait_sent(edges_out, edge_send.at[1])
    wait_sent(mixed_out, mixed_send.at[1])
    for band in range(PHASES):
        store(band).wait()


def local(pair, chain_index, norm_gain, norm_shift, w_in, b_in, w_out, b_out):
    weights = jnp.transpose(w_in, (0, 2, 1, 3))
    biases = jnp.transpose(b_in, (1, 0, 2))
    vmem = pl.BlockSpec(memory_space=pltpu.VMEM)
    smem = pl.BlockSpec(memory_space=pltpu.SMEM)
    anywhere = pl.BlockSpec(memory_space=pl.ANY)
    tile = (TILE_I, TILE_J, CH)
    updated = pl.pallas_call(
        kernel,
        out_shape=jax.ShapeDtypeStruct(tile, jnp.bfloat16),
        in_specs=[anywhere, vmem, smem] + [vmem] * 6,
        out_specs=anywhere,
        scratch_shapes=[
            pltpu.VMEM(tile, jnp.bfloat16),
            pltpu.VMEM(tile, jnp.bfloat16),
            pltpu.VMEM(tile, jnp.float32),
            pltpu.VMEM((2, CH * BAND, TILE_J), jnp.float32),
            pltpu.VMEM((DEVICES, 2, TILE_I, TILE_J), jnp.bfloat16),
            pltpu.VMEM((2, 2, ROWS, TILE_I, N), jnp.bfloat16),
            pltpu.VMEM((DEVICES, TILE_I, TILE_J), jnp.bfloat16),
            pltpu.VMEM((2, DEVICES, TILE_I, TILE_J), jnp.bfloat16),
            pltpu.VMEM((N // 256, N // 256, 256, 256), jnp.float32),
            pltpu.VMEM((2, 5, CH, CH), jnp.bfloat16),
            pltpu.VMEM((2, 4, CH, TILE_J), jnp.float32),
            pltpu.VMEM((2, 2, CH, TILE_J), jnp.float32),
            pltpu.SemaphoreType.DMA((PHASES,)),
            pltpu.SemaphoreType.DMA((2,)),
            pltpu.SemaphoreType.DMA((2, 2, PHASES)),
            pltpu.SemaphoreType.DMA((2,)),
            pltpu.SemaphoreType.DMA((2, PHASES)),
            pltpu.SemaphoreType.DMA((PHASES,)),
            pltpu.SemaphoreType.REGULAR,
        ],
        compiler_params=pltpu.CompilerParams(
            collective_id=1, has_side_effects=True, vmem_limit_bytes=56 << 20
        ),
        name="triangles",
    )(
        pair,
        chain_index.reshape(COLS, TILE_J),
        chain_index,
        norm_gain,
        norm_shift,
        weights,
        biases,
        w_out,
        b_out,
    )
    return settle(updated)


def settle_kernel(from_ref, to_ref):
    to_ref[...] = from_ref[...]


def settle(updated):
    block = pl.BlockSpec((TILE_I // 4, TILE_J, CH), lambda step: (step, 0, 0))
    return pl.pallas_call(
        settle_kernel,
        out_shape=jax.ShapeDtypeStruct(updated.shape, updated.dtype),
        grid=(4,),
        in_specs=[block],
        out_specs=block,
        name="settle",
    )(updated)


def solution(mesh):
    in_specs = (P("row", "col", None), P(), P(), P(), P(), P(), P(), P())
    out_specs = P("row", "col", None)
    return jax.shard_map(local, mesh=mesh, in_specs=in_specs, out_specs=out_specs, check_vma=False)
```

```python
import jax
import jax.numpy as jnp
from jax import lax
from jax.experimental import pallas as pl
from jax.experimental.pallas import tpu as pltpu
from jax.sharding import PartitionSpec as P

NCHAIN = 4
N = 1024
CH = 128
ROWS = 16
COLS = 8
DEVICES = ROWS * COLS
TILE_I = N // ROWS
TILE_J = N // COLS
PHASES = 4
BAND = TILE_I // PHASES
GROUP = 4
WIDE = GROUP * TILE_J
STRIDE = 97
MESH = pl.DeviceIdType.MESH
EPS = 1e-05


def partner(step, row, col):
    code = (STRIDE * step) & (DEVICES - 1)
    low, mid = code, code >> 2
    x = ((row >> 2) + low) & 3
    y = (col + mid + 2 * low) & 3
    z = (2 * (col >> 2) + ((row >> 1) & 1) + (code >> 4) + 2 * mid) & 3
    core = (row + (code >> 6)) & 1
    return 4 * x + 2 * (z & 1) + core, 4 * (z >> 1) + y


def dot(left, right, left_dim, right_dim):
    return lax.dot_general(
        left, right, (((left_dim,), (right_dim,)), ((), ())), preferred_element_type=jnp.float32
    )


def kernel(
    pair_ref,
    chain_lines_ref,
    chain_ref,
    gain_ref,
    shift_ref,
    w_in_ref,
    b_in_ref,
    w_out_ref,
    b_out_ref,
    out_ref,
    current,
    normed,
    gate,
    wide,
    edges_out,
    edges_in,
    mixed_out,
    mixed_in,
    partial,
    weights,
    b_column,
    hidden_column,
    load_sem,
    edge_send,
    edge_recv,
    mixed_send,
    mixed_recv,
    store_sem,
    ready_sem,
):
    row, col = lax.axis_index("row"), lax.axis_index("col")
    me = row * COLS + col
    barrier = pltpu.get_barrier_semaphore()
    average = jnp.full((CH, CH), 1.0 / CH, jnp.bfloat16)

    def band_rows(band):
        return pl.ds(pl.multiple_of(band * BAND, BAND), BAND)

    def load(band):
        rows = band_rows(band)
        return pltpu.make_async_copy(pair_ref.at[rows], current.at[rows], load_sem.at[band])

    def store(band):
        rows = band_rows(band)
        return pltpu.make_async_copy(current.at[rows], out_ref.at[rows], store_sem.at[band])

    for band in range(PHASES):
        load(band).start()

    def greet(sem, length, device):
        @pl.loop(1, length)
        def _(step):
            pl.semaphore_signal(sem, inc=1, device_id=device(step), device_id_type=MESH)

    greet(barrier, ROWS, lambda step: ((row + step) & (ROWS - 1), col))
    greet(barrier, COLS, lambda step: (row, (col + step) & (COLS - 1)))

    def column(values):
        return jnp.transpose(jnp.broadcast_to(values, (CH, CH)))

    for layer in range(2):
        for part in range(4):
            scale = 0.5 if part % 2 == 0 else 1.0
            b_column[layer, part] = column(b_in_ref[part, layer : layer + 1, :] * scale)
        for part in range(5):
            scale = 0.5 if part % 2 == 0 else 1.0
            turned = jnp.transpose(w_in_ref[layer, part].astype(jnp.float32)) * scale
            weights[layer, part] = turned.astype(jnp.bfloat16)
        hidden_column[layer, 0] = column(gain_ref[layer, 1:2, :])
        hidden_column[layer, 1] = column(shift_ref[layer, 1:2, :])

    def project(layer, band, halves, norm):
        col_half = jnp.where(chain_lines_ref[pl.ds(col, 1), :] < NCHAIN - 1, 0.5, 0.0)

        @pl.loop(0, BAND // GROUP)
        def _(step):
            first = band * BAND + step * GROUP
            lines = pl.ds(first, GROUP)
            if norm:
                values = current[lines].reshape(WIDE, CH)
                centred = values.astype(jnp.float32) - dot(values, average, 1, 0)
                spread = dot(jnp.square(centred).astype(jnp.bfloat16), average, 1, 0)
                values = centred * lax.rsqrt(spread + EPS) * gain_ref[layer, 0:1, :]
                values = (values + shift_ref[layer, 0:1, :]).astype(jnp.bfloat16)
                normed[lines] = values.reshape(GROUP, TILE_J, CH)
            else:
                values = normed[lines].reshape(WIDE, CH)
            masks = []
            for i in range(GROUP):
                chain = chain_ref[row * TILE_I + first + i]
                masks.append(col_half * jnp.where(chain < NCHAIN - 1, 1.0, 0.0))
            for half in halves:
                opening = dot(weights[layer, 2 * half], values, 1, 1)
                content = dot(weights[layer, 2 * half + 1], values, 1, 1)
                for i in range(GROUP):
                    at = slice(i * TILE_J, (i + 1) * TILE_J)
                    factor = jnp.tanh(opening[:, at] + b_column[layer, 2 * half]) + 1.0
                    gated = factor * (content[:, at] + b_column[layer, 2 * half + 1]) * masks[i]
                    wide[half, pl.ds(step * GROUP + i, CH, stride=BAND), :] = gated

        rows = band_rows(band)

        @pl.loop(0, CH // 32)
        def _(group):
            channels = pl.ds(pl.multiple_of(group * 32, 32), 32)
            source = pl.ds(pl.multiple_of(group * (32 * BAND), 32 * BAND), 32 * BAND)
            for half in halves:
                block = wide[half, source, :].astype(jnp.bfloat16).reshape(32, BAND, TILE_J)
                edges_out[channels, half, rows, :] = block

    def send_edges(layer, band, half):
        rows = band_rows(band)
        halves = slice(None) if half is None else half
        sem = edge_recv.at[layer, half or 0, band]
        place = edges_in.at[
            layer, halves, row, rows, pl.ds(pl.multiple_of(col * TILE_J, TILE_J), TILE_J)
        ]

        @pl.loop(1, DEVICES)
        def _(step):
            to_row, to_col = partner(step, row, col)
            pltpu.make_async_remote_copy(
                src_ref=edges_out.at[to_row * COLS + to_col, halves, rows, :],
                dst_ref=place,
                send_sem=edge_send.at[layer],
                recv_sem=sem,
                device_id=(to_row, to_col),
                device_id_type=MESH,
            ).start()

        pltpu.make_async_copy(edges_out.at[me, halves, rows, :], place, sem).start()

    def wait_edges(layer, band, half):
        halves = slice(None) if half is None else half
        whole = edges_in.at[layer, halves, :, band_rows(band), :]
        pltpu.make_async_copy(whole, whole, edge_recv.at[layer, half or 0, band]).wait()

    def wait_sent(buffer, sem):
        sent = buffer.at[pl.ds(0, DEVICES - 1)]
        pltpu.make_async_copy(sent, sent, sem).wait()

    def compute_gate(layer):
        @pl.loop(0, TILE_I // GROUP)
        def _(step):
            lines = pl.ds(step * GROUP, GROUP)
            logits = dot(normed[lines].reshape(WIDE, CH), weights[layer, 4], 1, 1)
            half = 0.5 * jnp.tanh(logits + 0.5 * b_in_ref[4, layer : layer + 1, :]) + 0.5
            gate[lines] = half.reshape(GROUP, TILE_J, CH)

    def contract_rows(band):
        rows = band_rows(band)
        left = edges_in[0, 0, :, rows, :].reshape(ROWS * BAND, N)

        @pl.loop(0, N // 256)
        def _(j):
            right = edges_in[0, 1, pl.ds(j * (256 // TILE_I), 256 // TILE_I)].reshape(256, N)
            mixed = dot(left, right, 1, 1).astype(jnp.bfloat16).reshape(ROWS, BAND, 256)
            for b in range(256 // TILE_J):
                lanes = slice(b * TILE_J, (b + 1) * TILE_J)
                for r in range(ROWS):
                    owner = r * COLS + j * (256 // TILE_J) + b
                    mixed_out[owner, rows, :] = mixed[r, :, lanes]

    def contract_columns(first, last):
        rows = slice(first * BAND, last * BAND)
        depth = ROWS * (last - first) * BAND

        @pl.loop(0, N // 256)
        def _(i):
            lanes = pl.ds(pl.multiple_of(i * 256, 256), 256)
            left = edges_in[1, 0, :, rows, lanes].reshape(depth, 256)
            for j in range(N // 256):
                right = edges_in[1, 1, :, rows, j * 256 : (j + 1) * 256].reshape(depth, 256)
                mixed = dot(left, right, 0, 0)
                if first:
                    mixed = mixed + partial[i, j]
                if last < PHASES:
                    partial[i, j] = mixed
                    continue
                mixed = mixed.astype(jnp.bfloat16)
                for a in range(256 // TILE_I):
                    for b in range(256 // TILE_J):
                        owner = (i * (256 // TILE_I) + a) * COLS + j * (256 // TILE_J) + b
                        mixed_out[owner] = mixed[
                            a * TILE_I : (a + 1) * TILE_I, b * TILE_J : (b + 1) * TILE_J
                        ]

    def send_mixed(layer, band):
        rows = band_rows(band)
        place = mixed_in.at[layer, me, rows, :]
        sem = mixed_recv.at[layer, band]

        @pl.loop(1, DEVICES)
        def _(step):
            to_row, to_col = partner(step, row, col)
            pltpu.make_async_remote_copy(
                src_ref=mixed_out.at[to_row * COLS + to_col, rows, :],
                dst_ref=place,
                send_sem=mixed_send.at[layer],
                recv_sem=sem,
                device_id=(to_row, to_col),
                device_id_type=MESH,
            ).start()

        pltpu.make_async_copy(mixed_out.at[me, rows, :], place, sem).start()

    def finish(layer, band):
        rows = band_rows(band)
        whole = mixed_in.at[layer, :, rows, :]
        pltpu.make_async_copy(whole, whole, mixed_recv.at[layer, band]).wait()

        @pl.loop(0, CH // 32)
        def _(group):
            channels = pl.ds(pl.multiple_of(group * 32, 32), 32)
            block = mixed_in[layer, channels, rows, :].astype(jnp.float32)
            target = pl.ds(pl.multiple_of(group * (32 * BAND), 32 * BAND), 32 * BAND)
            wide[0, target, :] = block.reshape(32 * BAND, TILE_J)

        @pl.loop(0, BAND // GROUP)
        def _(step):
            for i in range(GROUP):
                line = band * BAND + step * GROUP + i
                values = wide[0, pl.ds(step * GROUP + i, CH, stride=BAND), :]
                centred = values - jnp.mean(values, axis=0, keepdims=True)
                spread = jnp.mean(jnp.square(centred), axis=0, keepdims=True)
                hidden = centred * lax.rsqrt(spread + EPS) * hidden_column[layer, 0]
                hidden = (hidden + hidden_column[layer, 1]).astype(jnp.bfloat16)
                out = dot(hidden, w_out_ref[layer], 0, 0) + b_out_ref[layer : layer + 1, :]
                updated = current[line].astype(jnp.float32) + gate[line] * out
                current[line] = updated.astype(jnp.bfloat16)

    pl.semaphore_wait(barrier, ROWS - 1 + COLS - 1)
    greet(ready_sem, COLS, lambda step: (row, (col + step) & (COLS - 1)))

    @pl.loop(0, PHASES)
    def _(band):
        load(band).wait()
        project(0, band, (1,), True)

        @pl.when(band == 0)
        def _():
            pl.semaphore_wait(ready_sem, COLS - 1)

        send_edges(0, band, 1)

    @pl.loop(0, PHASES)
    def _(band):
        project(0, band, (0,), False)
        send_edges(0, band, 0)

    compute_gate(0)
    for band in range(PHASES):
        wait_edges(0, band, 1)

    @pl.loop(0, PHASES)
    def _(band):
        wait_edges(0, band, 0)
        contract_rows(band)
        send_mixed(0, band)

    wait_sent(edges_out, edge_send.at[0])

    @pl.loop(0, PHASES)
    def _(band):
        finish(0, band)
        project(1, band, (0, 1), True)
        send_edges(1, band, None)

    compute_gate(1)
    wait_sent(mixed_out, mixed_send.at[0])
    for band in range(PHASES - 1):
        wait_edges(1, band, None)
    contract_columns(0, PHASES - 1)
    wait_edges(1, PHASES - 1, None)
    contract_columns(PHASES - 1, PHASES)

    @pl.loop(0, PHASES)
    def _(band):
        send_mixed(1, band)

    @pl.loop(0, PHASES)
    def _(band):
        finish(1, band)
        store(band).start()

    wait_sent(edges_out, edge_send.at[1])
    wait_sent(mixed_out, mixed_send.at[1])
    for band in range(PHASES):
        store(band).wait()


def local(pair, chain_index, norm_gain, norm_shift, w_in, b_in, w_out, b_out):
    weights = jnp.transpose(w_in, (0, 2, 1, 3))
    biases = jnp.transpose(b_in, (1, 0, 2))
    vmem = pl.BlockSpec(memory_space=pltpu.VMEM)
    smem = pl.BlockSpec(memory_space=pltpu.SMEM)
    anywhere = pl.BlockSpec(memory_space=pl.ANY)
    tile = (TILE_I, TILE_J, CH)
    return pl.pallas_call(
        kernel,
        out_shape=jax.ShapeDtypeStruct(tile, jnp.bfloat16),
        in_specs=[anywhere, vmem, smem] + [vmem] * 6,
        out_specs=anywhere,
        scratch_shapes=[
            pltpu.VMEM(tile, jnp.bfloat16),
            pltpu.VMEM(tile, jnp.bfloat16),
            pltpu.VMEM(tile, jnp.float32),
            pltpu.VMEM((2, CH * BAND, TILE_J), jnp.float32),
            pltpu.VMEM((DEVICES, 2, TILE_I, TILE_J), jnp.bfloat16),
            pltpu.VMEM((2, 2, ROWS, TILE_I, N), jnp.bfloat16),
            pltpu.VMEM((DEVICES, TILE_I, TILE_J), jnp.bfloat16),
            pltpu.VMEM((2, DEVICES, TILE_I, TILE_J), jnp.bfloat16),
            pltpu.VMEM((N // 256, N // 256, 256, 256), jnp.float32),
            pltpu.VMEM((2, 5, CH, CH), jnp.bfloat16),
            pltpu.VMEM((2, 4, CH, TILE_J), jnp.float32),
            pltpu.VMEM((2, 2, CH, TILE_J), jnp.float32),
            pltpu.SemaphoreType.DMA((PHASES,)),
            pltpu.SemaphoreType.DMA((2,)),
            pltpu.SemaphoreType.DMA((2, 2, PHASES)),
            pltpu.SemaphoreType.DMA((2,)),
            pltpu.SemaphoreType.DMA((2, PHASES)),
            pltpu.SemaphoreType.DMA((PHASES,)),
            pltpu.SemaphoreType.REGULAR,
        ],
        compiler_params=pltpu.CompilerParams(
            collective_id=1, has_side_effects=True, vmem_limit_bytes=56 << 20
        ),
        name="triangles",
    )(
        pair,
        chain_index.reshape(COLS, TILE_J),
        chain_index,
        norm_gain,
        norm_shift,
        weights,
        biases,
        w_out,
        b_out,
    )


def solution(mesh):
    in_specs = (P("row", "col", None), P(), P(), P(), P(), P(), P(), P())
    out_specs = P("row", "col", None)
    return jax.shard_map(local, mesh=mesh, in_specs=in_specs, out_specs=out_specs, check_vma=False)
```
